32 devices in a mesh: row: 4 (over x, core), col: 2 (over y), tm: 4 (over z).
Axes of the slice: x: 2, y: 2, z: 4, core: 2. Of those that a mesh axis runs over, the one named last changes fastest.
Arguments:
- right_sides: bfloat16 [8, 256, 16384], P(None, 'tm', ('row', 'col')), may hold values from -6 to 6
- eigen_basis: bfloat16 [16384, 16384], P('row', 'col'), may hold values from -0.046875 to 0.046875
- space_values: float32 [16384], P('col'), may hold values from 0.02 to 4
- time_basis: bfloat16 [256, 256], replicated, may hold values from -0.375 to 0.375
- time_values: float32 [256], replicated, may hold values from 0.05 to 4
- noise_level: float32 [1], replicated, may hold values from 0.05 to 0.5
Outputs:
- solved: float32 [8, 256, 16384], P(None, 'tm', ('row', 'col'))
The draws below stay inside these ranges and needn't reach their ends.
All inputs are finite; a program needn't handle non-finite values.
Results may differ from the reference program's by a relative error of at most 0.0037.
Values may be sent and summed in bfloat16 or wider, within the bound.
A program may use at most 192 MiB of HBM per device.

```python
import math
import jax
import jax.numpy as jnp

NS = 16384
NT = 256
RHS = 8


def shard_levels(key, dims, pieces, low, high):
    factor_of, own = 1.0, jax.random.fold_in(key, 6)
    for dim, parts in pieces:
        steps = jnp.exp(jax.random.uniform(jax.random.fold_in(own, dim), (parts,), jnp.float32, low / len(pieces), high / len(pieces)))
        factor_of = factor_of * jnp.repeat(steps, dims[dim] // parts).reshape([-1 if axis == dim else 1 for axis in range(len(dims))])
    return factor_of


def normal_values(own_key, dims, spread, reach, pieces=(), held_as=jnp.bfloat16):
    entries = jax.random.normal(own_key, dims, jnp.float32) * spread
    if len(pieces) > 0:
        entries = shard_levels(own_key, dims, pieces, -0.22, 0.18) * entries
    return jnp.clip(entries, min=-reach, max=reach).astype(held_as)


def setup_inputs(seed: int = 0) -> dict:
    streams_of = jax.random.split(jax.random.key(seed), 7)
    right_sides = normal_values(streams_of[0], (RHS, NT, NS), 1.0, 6.0, ((1, 4), (2, 8)))
    eigen_basis = normal_values(streams_of[1], (NS, NS), NS ** -0.5, 0.046875, ((0, 4), (1, 2)))
    space_values = jnp.clip(jnp.exp(math.log(4.0) - 5.2983174 * jax.random.uniform(streams_of[2], (NS,), jnp.float32) ** shard_levels(streams_of[2], (NS,), ((0, 2),), -0.2, 0.2)), 0.02, 4.0)
    time_basis = normal_values(streams_of[3], (NT, NT), NT ** -0.5, 0.375)
    time_values = jnp.clip(jnp.exp(jax.random.uniform(streams_of[4], (NT,), jnp.float32, math.log(0.05), math.log(4.0))), 0.05, 4.0)
    noise_level = jnp.clip(jax.random.uniform(streams_of[5], (1,), jnp.float32, 0.05, 0.5), 0.05, 0.5)
    return {"right_sides": right_sides, "eigen_basis": eigen_basis, "space_values": space_values, "time_basis": time_basis, "time_values": time_values, "noise_level": noise_level}


def reference(right_sides, eigen_basis, space_values, time_basis, time_values, noise_level):
    flat = right_sides.reshape(RHS * NT, NS)
    spectral = jnp.dot(flat, eigen_basis, preferred_element_type=jnp.float32).astype(jnp.bfloat16)
    spectral = spectral.reshape(RHS, NT, NS)
    mixed = jnp.einsum("tj,rti->rji", time_basis.astype(jnp.float32), spectral.astype(jnp.float32))
    denom = space_values[None, None, :] * time_values[None, :, None] + noise_level[0]
    scaled = (mixed / denom).astype(jnp.bfloat16)
    back_time = jnp.einsum("tj,rji->rti", time_basis.astype(jnp.float32), scaled.astype(jnp.float32)).astype(jnp.bfloat16)
    solved = jnp.dot(back_time.reshape(RHS * NT, NS), eigen_basis.T, preferred_element_type=jnp.float32)
    return solved.reshape(RHS, NT, NS)
```

```python
import functools

import jax
import jax.numpy as jnp
from jax import lax
from jax.experimental import pallas as pl
from jax.experimental.pallas import tpu as pltpu
from jax.sharding import PartitionSpec as P

BF16 = jnp.bfloat16
F32 = jnp.float32
ROW_PARTS = 2
BASIS_PARTS = 2


def dot(a, b, dims):
    return lax.dot_general(a, b, (dims, ((), ())), preferred_element_type=F32)


def filter_kernel(fields, span, steps, noise_ref, value_ref, level_ref, basis_ref, *refs):
    ins, outs = refs[:steps], refs[steps:]
    denom = level_ref[...] * value_ref[...] + noise_ref[0]
    for r in range(fields):
        rows = slice(r * span, (r + 1) * span)
        block = jnp.concatenate([ref[rows, :] for ref in ins], axis=0)
        mixed = dot(basis_ref[...], block, ((0,), (0,)))
        scaled = (mixed / denom).astype(BF16)
        back = dot(basis_ref[...], scaled, ((1,), (0,))).astype(BF16)
        for d in range(steps):
            outs[d][rows, :] = back[d * span : (d + 1) * span, :]


def time_filter(fields, span, blocks, values, levels, basis, noise):
    steps = len(blocks)
    return pl.pallas_call(
        functools.partial(filter_kernel, fields, span, steps),
        out_shape=[jax.ShapeDtypeStruct(b.shape, b.dtype) for b in blocks],
        in_specs=[pl.BlockSpec(memory_space=pltpu.SMEM)]
        + [pl.BlockSpec(memory_space=pltpu.VMEM)] * (3 + steps),
        out_specs=[pl.BlockSpec(memory_space=pltpu.VMEM)] * steps,
        compiler_params=pltpu.CompilerParams(vmem_limit_bytes=24 * 1024 * 1024),
        cost_estimate=pl.CostEstimate(
            flops=4 * fields * basis.shape[0] * basis.shape[1] * blocks[0].shape[1],
            bytes_accessed=4 * steps * blocks[0].size,
            transcendentals=0,
        ),
    )(noise, values, levels, basis, *blocks)


def shift(x, axis, by):
    n = lax.axis_size(axis)
    return lax.ppermute(x, axis, [(i, (i + by) % n) for i in range(n)])


def part(x, index, width):
    return lax.dynamic_slice_in_dim(x, index * width, width, 1)


def shards(right_sides, eigen_basis, space_values, time_basis, time_values, noise_level):
    fields, span, own_sites = right_sides.shape
    rows, cols, tms = lax.axis_size("row"), lax.axis_size("col"), lax.axis_size("tm")
    chips = rows // 2
    me_row, me_col, me_tm = lax.axis_index("row"), lax.axis_index("col"), lax.axis_index("tm")
    core, chip = me_row % 2, me_row // 2
    basis_count = eigen_basis.shape[1]
    group = fields // ROW_PARTS
    lines = group * span
    wide = basis_count // BASIS_PARTS
    half = wide // 2
    quarter = half // chips
    piece = quarter // tms
    basis_turned = jnp.concatenate(
        [
            lax.dynamic_slice_in_dim(time_basis, ((me_tm - d) % tms) * span, span, 0)
            for d in range(tms)
        ],
        axis=0,
    )
    levels = time_values.reshape(-1, 1)
    flip_core = [(i, i ^ 1) for i in range(rows)]

    def to_chip(x, by):
        return lax.ppermute(x, "row", [(i, (i + 2 * by) % rows) for i in range(rows)])

    def place(whole, x, index):
        return lax.dynamic_update_slice_in_dim(whole, x, index * x.shape[1], 1)

    outs = []
    gathered = []
    for k in range(ROW_PARTS):
        mine = right_sides[k * group : (k + 1) * group].reshape(lines, own_sites)
        whole = jnp.zeros((lines, own_sites * cols), BF16)
        whole = place(whole, mine, me_col)
        for d in range(1, cols):
            whole = place(whole, shift(mine, "col", d), (me_col - d) % cols)
        gathered.append(whole)

    for k in range(ROW_PARTS):
        total = None
        for c in range(BASIS_PARTS):
            columns = eigen_basis[:, c * wide : (c + 1) * wide]
            partial = dot(gathered[k], columns, ((1,), (0,)))
            sent = part(partial, 1 - core, half).astype(BF16)
            near = part(partial, core, half) + lax.ppermute(sent, "row", flip_core).astype(F32)
            spectral = part(near, chip, quarter)
            for d in range(1, chips):
                far = part(near, (chip + d) % chips, quarter).astype(BF16)
                spectral = spectral + to_chip(far, d).astype(F32)
            spectral = spectral.astype(BF16)
            blocks = [part(spectral, me_tm, piece)]
            for d in range(1, tms):
                blocks.append(shift(part(spectral, (me_tm + d) % tms, piece), "tm", d))
            start = c * wide + core * half + chip * quarter + me_tm * piece
            values = lax.dynamic_slice_in_dim(space_values, start, piece, 0).reshape(1, piece)
            blocks = time_filter(group, span, blocks, values, levels, basis_turned, noise_level)
            own = jnp.zeros((lines, quarter), BF16)
            own = place(own, blocks[0], me_tm)
            for d in range(1, tms):
                own = place(own, shift(blocks[d], "tm", -d), (me_tm + d) % tms)
            side = place(jnp.zeros((lines, half), BF16), own, chip)
            for d in range(1, chips):
                side = place(side, to_chip(own, d), (chip - d) % chips)
            other = lax.ppermute(side, "row", flip_core)
            both = place(place(jnp.zeros((lines, wide), BF16), side, core), other, 1 - core)
            terms = dot(both, columns, ((1,), (1,)))
            total = terms if total is None else total + terms
        result = part(total, me_col, own_sites)
        for d in range(1, cols):
            sent = part(total, (me_col + d) % cols, own_sites).astype(BF16)
            result = result + shift(sent, "col", d).astype(F32)
        outs.append(result.reshape(group, span, own_sites))
    return jnp.concatenate(outs, axis=0)


def solution(mesh):
    placed = (P(None, "tm", ("row", "col")), P("row", "col"), P("col"), P(), P(), P())
    return jax.shard_map(
        shards, mesh=mesh, in_specs=placed, out_specs=P(None, "tm", ("row", "col")), check_vma=False
    )
```

```python
import functools

import jax
import jax.numpy as jnp
from jax import lax
from jax.experimental import pallas as pl
from jax.experimental.pallas import tpu as pltpu
from jax.sharding import PartitionSpec as P

BF16 = jnp.bfloat16
F32 = jnp.float32
PASSES = 2
MOST_PARTS = 8
LEAST_WIDE = 512
TILE = 256
STRIPS = 4
SEMS = 4
DEPTH = 6


def dot(a, b, dims):
    return lax.dot_general(a, b, (dims, ((), ())), preferred_element_type=F32)


def kernel(
    cols, tms, span, parts,
    noise, values, levels, basis, fields, eigen, out,
    sites, acc, e1, e2, near, core_out, core_in, mid, x_out, x_in, z_out, z_in,
    b_out, back, y_out, y_in,
    e1_sem, e2_sem, c1_s, c1_r, x1_s, x1_r, z1_s, z1_r, z2_s, z2_r, x2_s, x2_r, c2_s, c2_r,
    g_s, g_r, y_s, y_r,
):
    row, col, tm = lax.axis_index("row"), lax.axis_index("col"), lax.axis_index("tm")
    core, chip = lax.rem(row, 2), lax.div(row, 2)
    other_core = {"row": chip * 2 + (1 - core)}
    other_chip = {"row": (1 - chip) * 2 + core}
    lines = sites.shape[1]
    own = fields.shape[1]
    wide = back.shape[2]
    half, quarter = wide // 2, wide // 4
    strip = eigen.shape[0] // STRIPS
    count = PASSES * parts
    tiles = wide // TILE
    group = lines // tms

    def at(base, size):
        return pl.ds(pl.multiple_of(base, 128), size)

    def rows_at(base, size):
        return pl.ds(pl.multiple_of(base, 16), size)

    def remote(src, dst, send, recv, to):
        return pltpu.make_async_remote_copy(
            src_ref=src, dst_ref=dst, send_sem=send, recv_sem=recv,
            device_id=to, device_id_type=pl.DeviceIdType.MESH,
        )

    barrier = pltpu.get_barrier_semaphore()
    friends = [other_core, other_chip]
    friends += [{"tm": lax.rem(tm + d, tms)} for d in range(1, tms)]
    friends += [{"col": lax.rem(col + d, cols)} for d in range(1, cols)]
    for friend in friends:
        pl.semaphore_signal(barrier, inc=1, device_id=friend, device_id_type=pl.DeviceIdType.MESH)
    pl.semaphore_wait(barrier, len(friends))

    def gather(p, d):
        return remote(
            fields.at[pl.ds(p * lines, lines), :],
            sites.at[p, :, at(col * own, own)],
            g_s.at[p, d - 1], g_r.at[p, d - 1],
            {"col": lax.rem(col + d, cols)},
        )

    def scatter(p, d):
        return remote(
            y_out.at[p, d - 1], y_in.at[p, d - 1], y_s.at[p, d - 1], y_r.at[p, d - 1],
            {"col": lax.rem(col + d, cols)},
        )

    def c1(c):
        m = lax.rem(c, SEMS)
        return remote(core_out, core_in.at[c], c1_s.at[m], c1_r.at[m], other_core)

    def x1(c):
        m = lax.rem(c, SEMS)
        return remote(x_out, x_in.at[c], x1_s.at[m], x1_r.at[m], other_chip)

    def z1(c, d):
        m = lax.rem(c, SEMS)
        to = lax.rem(tm + d, tms)
        return remote(
            z_out.at[rows_at(to * group, group), :], z_in.at[c, tm],
            z1_s.at[m, d - 1], z1_r.at[m, d - 1], {"tm": to},
        )

    my_quarter = core * half + chip * quarter

    def z2(c, d):
        m = lax.rem(c, SEMS)
        to = lax.rem(tm + d, tms)
        return remote(
            b_out.at[to],
            back.at[c, rows_at(tm * group, group), at(my_quarter, quarter)],
            z2_s.at[m, d - 1], z2_r.at[m, d - 1], {"tm": to},
        )

    def x2(c):
        m = lax.rem(c, SEMS)
        place = back.at[c, :, at(my_quarter, quarter)]
        return remote(place, place, x2_s.at[m], x2_r.at[m], other_chip)

    def c2(c):
        m = lax.rem(c, SEMS)
        place = back.at[c, :, at(core * half, half)]
        return remote(place, place, c2_s.at[m], c2_r.at[m], other_core)

    def tile_start(j):
        per = tiles // 2
        side = (1 - core) if j < per else core
        return side * half + (j % per) * TILE

    def fetch1(c, j):
        first = lax.rem(c, parts) * wide + tile_start(j)
        return pltpu.make_async_copy(eigen.at[:, at(first, TILE)], e1.at[j % 2], e1_sem.at[j % 2])

    def fetch2(c, j):
        first = lax.rem(c, parts) * wide
        return pltpu.make_async_copy(
            eigen.at[pl.ds(j * strip, strip), at(first, wide)], e2.at[j % 2], e2_sem.at[j % 2]
        )

    for d in range(1, cols):
        gather(0, d).start()
    for p in range(PASSES):
        sites[p, :, at(col * own, own)] = fields[pl.ds(p * lines, lines), :]

    def step(s, carry):
        @pl.when(s < count)
        def _():
            fetch1(s, 0).start()
            fetch1(s, 1).start()

        @pl.when(s >= DEPTH)
        def _():
            fetch2(s - DEPTH, 0).start()
            fetch2(s - DEPTH, 1).start()

        @pl.when((s >= 5) & (s - 5 < count))
        def _():
            x2(s - 5).wait()
            c2(s - 5).start()

        @pl.when((s >= 4) & (s - 4 < count))
        def _():
            for d in range(1, tms):
                z2(s - 4, d).wait()
            x2(s - 4).start()

        @pl.when((s >= 3) & (s - 3 < count))
        def _():
            c = s - 3
            for d in range(1, tms):
                z1(c, d).wait()
            first = lax.rem(c, parts) * wide + my_quarter
            denom = levels[...] * values[:, at(first, quarter)] + noise[0]
            for r in range(group // span):
                lines_r = slice(r * span, (r + 1) * span)
                block = jnp.concatenate([z_in[c, j, lines_r, :] for j in range(tms)], axis=0)
                mixed = dot(basis[...], block, ((0,), (0,)))
                scaled = (mixed / denom).astype(BF16)
                result = dot(basis[...], scaled, ((1,), (0,))).astype(BF16)
                for j in range(tms):
                    b_out[j, lines_r, :] = result[j * span : (j + 1) * span, :]
            for d in range(1, tms):
                z2(c, d).start()
            back[c, rows_at(tm * group, group), at(my_quarter, quarter)] = b_out[tm]

        @pl.when((s >= 2) & (s - 2 < count))
        def _():
            c = s - 2
            x1(c).wait()
            z_out[...] = (mid[...] + x_in[c].astype(F32)).astype(BF16)
            for d in range(1, tms):
                z1(c, d).start()
            z_in[c, tm] = z_out[rows_at(tm * group, group), :]

        @pl.when((s >= 1) & (s - 1 < count))
        def _():
            c = s - 1
            c1(c).wait()
            far = at((1 - chip) * quarter, quarter)
            mine = at(chip * quarter, quarter)
            x_out[...] = (near[:, far] + core_in[c, :, far].astype(F32)).astype(BF16)
            x1(c).start()
            mid[...] = near[:, mine] + core_in[c, :, mine].astype(F32)

        @pl.when(s < count)
        def _():
            p = lax.div(s, parts)
            for q in range(PASSES):
                @pl.when(s == q * parts)
                def _():
                    for d in range(1, cols):
                        gather(q, d).wait()
                    if q + 1 < PASSES:
                        for d in range(1, cols):
                            gather(q + 1, d).start()

            for j in range(tiles):
                fetch1(s, j).wait()
                product = dot(sites[p], e1[j % 2], ((1,), (0,)))
                if j + 2 < tiles:
                    fetch1(s, j + 2).start()
                first = (j % (tiles // 2)) * TILE
                if j < tiles // 2:
                    core_out[:, first : first + TILE] = product.astype(BF16)
                else:
                    near[:, first : first + TILE] = product
                if j == tiles // 2 - 1:
                    c1(s).start()

        @pl.when(s >= DEPTH)
        def _():
            c = s - DEPTH
            c2(c).wait()

            @pl.when(lax.rem(c, parts) == 0)
            def _():
                acc[...] = jnp.zeros_like(acc)

            for j in range(STRIPS):
                fetch2(c, j).wait()
                acc[:, j * strip : (j + 1) * strip] += dot(back[c], e2[j % 2], ((1,), (1,)))
                if j + 2 < STRIPS:
                    fetch2(c, j + 2).start()
            for q in range(PASSES):
                @pl.when(c == (q + 1) * parts - 1)
                def _():
                    for d in range(1, cols):
                        to = lax.rem(col + d, cols)
                        y_out[q, d - 1] = acc[:, at(to * own, own)].astype(BF16)
                        scatter(q, d).start()
                    out[q * lines : (q + 1) * lines, :] = acc[:, at(col * own, own)]

        return carry

    lax.fori_loop(0, count + DEPTH, step, 0)
    for p in range(PASSES):
        for d in range(1, cols):
            scatter(p, d).wait()
            out[p * lines : (p + 1) * lines, :] += y_in[p, d - 1].astype(F32)


def shards(right_sides, eigen_basis, space_values, time_basis, time_values, noise_level):
    count, span, own = right_sides.shape
    cols, tms = lax.axis_size("col"), lax.axis_size("tm")
    lines = count * span // PASSES
    depth, width = eigen_basis.shape
    parts = min(MOST_PARTS, width // LEAST_WIDE)
    wide = width // parts
    half, quarter = wide // 2, wide // 4
    group = lines // tms
    chunks = PASSES * parts
    dma = pltpu.SemaphoreType.DMA
    vmem = pl.BlockSpec(memory_space=pltpu.VMEM)
    result = pl.pallas_call(
        functools.partial(kernel, cols, tms, span, parts),
        out_shape=jax.ShapeDtypeStruct((count * span, own), F32),
        in_specs=[pl.BlockSpec(memory_space=pltpu.SMEM), vmem, vmem, vmem, vmem]
        + [pl.BlockSpec(memory_space=pl.ANY)],
        out_specs=vmem,
        scratch_shapes=[
            pltpu.VMEM((PASSES, lines, depth), BF16),
            pltpu.VMEM((lines, depth), F32),
            pltpu.VMEM((2, depth, TILE), BF16),
            pltpu.VMEM((2, depth // STRIPS, wide), BF16),
            pltpu.VMEM((lines, half), F32),
            pltpu.VMEM((lines, half), BF16),
            pltpu.VMEM((chunks, lines, half), BF16),
            pltpu.VMEM((lines, quarter), F32),
            pltpu.VMEM((lines, quarter), BF16),
            pltpu.VMEM((chunks, lines, quarter), BF16),
            pltpu.VMEM((lines, quarter), BF16),
            pltpu.VMEM((chunks, tms, group, quarter), BF16),
            pltpu.VMEM((tms, group, quarter), BF16),
            pltpu.VMEM((chunks, lines, wide), BF16),
            pltpu.VMEM((PASSES, cols - 1, lines, own), BF16),
            pltpu.VMEM((PASSES, cols - 1, lines, own), BF16),
            dma((2,)), dma((2,)),
            dma((SEMS,)), dma((SEMS,)), dma((SEMS,)), dma((SEMS,)),
            dma((SEMS, tms - 1)), dma((SEMS, tms - 1)),
            dma((SEMS, tms - 1)), dma((SEMS, tms - 1)),
            dma((SEMS,)), dma((SEMS,)), dma((SEMS,)), dma((SEMS,)),
            dma((PASSES, cols - 1)), dma((PASSES, cols - 1)),
            dma((PASSES, cols - 1)), dma((PASSES, cols - 1)),
        ],
        compiler_params=pltpu.CompilerParams(
            collective_id=0, has_side_effects=True, vmem_limit_bytes=60 * 1024 * 1024
        ),
        cost_estimate=pl.CostEstimate(
            flops=4 * count * span * depth * width,
            bytes_accessed=4 * PASSES * depth * width,
            transcendentals=0,
        ),
    )(
        noise_level, space_values.reshape(1, -1), time_values.reshape(-1, 1), time_basis,
        right_sides.reshape(count * span, own), eigen_basis,
    )
    return result.reshape(count, span, own)


def solution(mesh):
    placed = (P(None, "tm", ("row", "col")), P("row", "col"), P("col"), P(), P(), P())
    return jax.shard_map(
        shards, mesh=mesh, in_specs=placed, out_specs=P(None, "tm", ("row", "col")), check_vma=False
    )
```

```python
import functools

import jax
import jax.numpy as jnp
from jax import lax
from jax.experimental import pallas as pl
from jax.experimental.pallas import tpu as pltpu
from jax.sharding import PartitionSpec as P

BF16 = jnp.bfloat16
F32 = jnp.float32
PASSES = 2
MOST_PARTS = 8
LEAST_WIDE = 512
TILE = 256
STRIP = 1024
SEMS = 4
DEPTH = 6


def dot(a, b, dims):
    return lax.dot_general(a, b, (dims, ((), ())), preferred_element_type=F32)


def kernel(
    cols, tms, span, parts,
    noise, values, levels, basis, fields, eigen, out,
    sites, pre, acc, e1, e2, near, core_out, core_in, mid, x_out, x_in, z_out, z_in,
    b_out, back, y_out, y_in,
    e1_sem, e2_sem, c1_s, c1_r, x1_s, x1_r, z1_s, z1_r, z2_s, z2_r, x2_s, x2_r, c2_s, c2_r,
    g_s, g_r, y_s, y_r,
):
    row, col, tm = lax.axis_index("row"), lax.axis_index("col"), lax.axis_index("tm")
    core, chip = lax.rem(row, 2), lax.div(row, 2)
    other_core = {"row": chip * 2 + (1 - core)}
    other_chip = {"row": (1 - chip) * 2 + core}
    lines = acc.shape[0]
    own = fields.shape[1]
    wide = back.shape[2]
    half, quarter = wide // 2, wide // 4
    strip = e2.shape[1]
    strips = own // strip
    count = PASSES * parts
    tiles = wide // TILE
    group = lines // tms

    def at(base, size):
        return pl.ds(pl.multiple_of(base, 128), size)

    def rows_at(base, size):
        return pl.ds(pl.multiple_of(base, 16), size)

    def remote(src, dst, send, recv, to):
        return pltpu.make_async_remote_copy(
            src_ref=src, dst_ref=dst, send_sem=send, recv_sem=recv,
            device_id=to, device_id_type=pl.DeviceIdType.MESH,
        )

    barrier = pltpu.get_barrier_semaphore()
    friends = [other_core, other_chip]
    friends += [{"tm": lax.rem(tm + d, tms)} for d in range(1, tms)]
    friends += [{"col": lax.rem(col + d, cols)} for d in range(1, cols)]
    for friend in friends:
        pl.semaphore_signal(barrier, inc=1, device_id=friend, device_id_type=pl.DeviceIdType.MESH)
    pl.semaphore_wait(barrier, len(friends))

    def gather(p, d):
        return remote(
            fields.at[pl.ds(p * lines, lines), :],
            sites.at[p, d - 1],
            g_s.at[p, d - 1], g_r.at[p, d - 1],
            {"col": lax.rem(col + d, cols)},
        )

    def scatter(p, d):
        return remote(
            y_out.at[p, d - 1], y_in.at[p, d - 1], y_s.at[p, d - 1], y_r.at[p, d - 1],
            {"col": lax.rem(col + d, cols)},
        )

    def c1(c):
        m = lax.rem(c, SEMS)
        return remote(core_out, core_in.at[c], c1_s.at[m], c1_r.at[m], other_core)

    def x1(c):
        m = lax.rem(c, SEMS)
        return remote(x_out, x_in.at[c], x1_s.at[m], x1_r.at[m], other_chip)

    def z1(c, d):
        m = lax.rem(c, SEMS)
        to = lax.rem(tm + d, tms)
        return remote(
            z_out.at[rows_at(to * group, group), :], z_in.at[c, tm],
            z1_s.at[m, d - 1], z1_r.at[m, d - 1], {"tm": to},
        )

    my_quarter = core * half + chip * quarter

    def z2(c, d):
        m = lax.rem(c, SEMS)
        to = lax.rem(tm + d, tms)
        return remote(
            b_out.at[to],
            back.at[c, rows_at(tm * group, group), at(my_quarter, quarter)],
            z2_s.at[m, d - 1], z2_r.at[m, d - 1], {"tm": to},
        )

    def x2(c):
        m = lax.rem(c, SEMS)
        place = back.at[c, :, at(my_quarter, quarter)]
        return remote(place, place, x2_s.at[m], x2_r.at[m], other_chip)

    def c2(c):
        m = lax.rem(c, SEMS)
        place = back.at[c, :, at(core * half, half)]
        return remote(place, place, c2_s.at[m], c2_r.at[m], other_core)

    def tile_start(j):
        per = tiles // 2
        side = (1 - core) if j < per else core
        return side * half + (j % per) * TILE

    def fetch1(c, j, d):
        first = lax.rem(c, parts) * wide + tile_start(j)
        block = lax.rem(col - d + cols, cols)
        return pltpu.make_async_copy(
            eigen.at[rows_at(block * own, own), at(first, TILE)],
            e1.at[j % 2, d], e1_sem.at[j % 2, d],
        )

    def fetch2(c, j):
        first = lax.rem(c, parts) * wide
        block = lax.rem(col + 1 + j // strips, cols)
        return pltpu.make_async_copy(
            eigen.at[rows_at(block * own + (j % strips) * strip, strip), at(first, wide)],
            e2.at[j % 2], e2_sem.at[j % 2],
        )

    def fetch_head(t):
        slot = lax.rem(t, 2)
        return pltpu.make_async_copy(
            eigen.at[rows_at(col * own, own), at(t * TILE, TILE)],
            e1.at[slot, 0], e1_sem.at[slot, 0],
        )

    def fetch_tail(t):
        slot = lax.rem(t, 2)
        k, i = lax.div(t, strips), lax.rem(t, strips)
        return pltpu.make_async_copy(
            eigen.at[rows_at(col * own + i * strip, strip), at(k * wide, wide)],
            e2.at[slot], e2_sem.at[slot],
        )

    heads, tails = parts * tiles, parts * strips

    for d in range(1, cols):
        gather(0, d).start()
    fetch_head(0).start()
    fetch_head(1).start()

    def head(t, carry):
        fetch_head(t).wait()
        pre[:, at(t * TILE, TILE)] = dot(fields[0:lines, :], e1[lax.rem(t, 2), 0], ((1,), (0,)))

        @pl.when(t + 2 < heads)
        def _():
            fetch_head(t + 2).start()

        return carry

    lax.fori_loop(0, heads, head, 0)
    others = (cols - 1) * strips

    def project(s, q):
        lo = 1 if q == 0 else 0
        for j in range(tiles):
            product = None
            if q == 0:
                product = pre[:, at(lax.rem(s, parts) * wide + tile_start(j), TILE)]
            for d in range(lo, cols):
                fetch1(s, j, d).wait()
                left = fields[q * lines : (q + 1) * lines, :] if d == 0 else sites[q, d - 1]
                term = dot(left, e1[j % 2, d], ((1,), (0,)))
                product = term if product is None else product + term
            if j + 2 < tiles:
                for d in range(lo, cols):
                    fetch1(s, j + 2, d).start()
            first = (j % (tiles // 2)) * TILE
            if j < tiles // 2:
                core_out[:, first : first + TILE] = product.astype(BF16)
            else:
                near[:, first : first + TILE] = product
            if j == tiles // 2 - 1:
                c1(s).start()

    def step(s, carry):
        for q in range(PASSES):
            @pl.when((s >= q * parts) & (s < (q + 1) * parts))
            def _():
                for j in range(2):
                    for d in range(1 if q == 0 else 0, cols):
                        fetch1(s, j, d).start()

        @pl.when(s >= DEPTH)
        def _():
            for j in range(min(2, others)):
                fetch2(s - DEPTH, j).start()

        @pl.when((s >= 5) & (s - 5 < count))
        def _():
            x2(s - 5).wait()
            c2(s - 5).start()

        @pl.when((s >= 4) & (s - 4 < count))
        def _():
            for d in range(1, tms):
                z2(s - 4, d).wait()
            x2(s - 4).start()

        @pl.when((s >= 3) & (s - 3 < count))
        def _():
            c = s - 3
            for d in range(1, tms):
                z1(c, d).wait()
            first = lax.rem(c, parts) * wide + my_quarter
            denom = levels[...] * values[:, at(first, quarter)] + noise[0]
            for r in range(group // span):
                lines_r = slice(r * span, (r + 1) * span)
                block = jnp.concatenate([z_in[c, j, lines_r, :] for j in range(tms)], axis=0)
                mixed = dot(basis[...], block, ((0,), (0,)))
                scaled = (mixed / denom).astype(BF16)
                result = dot(basis[...], scaled, ((1,), (0,))).astype(BF16)
                for j in range(tms):
                    b_out[j, lines_r, :] = result[j * span : (j + 1) * span, :]
            for d in range(1, tms):
                z2(c, d).start()
            back[c, rows_at(tm * group, group), at(my_quarter, quarter)] = b_out[tm]

        @pl.when((s >= 2) & (s - 2 < count))
        def _():
            c = s - 2
            x1(c).wait()
            z_out[...] = (mid[...] + x_in[c].astype(F32)).astype(BF16)
            for d in range(1, tms):
                z1(c, d).start()
            z_in[c, tm] = z_out[rows_at(tm * group, group), :]

        @pl.when((s >= 1) & (s - 1 < count))
        def _():
            c = s - 1
            c1(c).wait()
            far = at((1 - chip) * quarter, quarter)
            mine = at(chip * quarter, quarter)
            x_out[...] = (near[:, far] + core_in[c, :, far].astype(F32)).astype(BF16)
            x1(c).start()
            mid[...] = near[:, mine] + core_in[c, :, mine].astype(F32)

        for q in range(PASSES):
            @pl.when(s == q * parts)
            def _():
                for d in range(1, cols):
                    gather(q, d).wait()
                if q + 1 < PASSES:
                    for d in range(1, cols):
                        gather(q + 1, d).start()

            @pl.when((s >= q * parts) & (s < (q + 1) * parts))
            def _():
                project(s, q)

        @pl.when(s >= DEPTH)
        def _():
            c = s - DEPTH
            c2(c).wait()

            @pl.when(lax.rem(c, parts) == 0)
            def _():
                acc[...] = jnp.zeros_like(acc)

            for j in range(others):
                fetch2(c, j).wait()
                acc[:, j * strip : (j + 1) * strip] += dot(back[c], e2[j % 2], ((1,), (1,)))
                if j + 2 < others:
                    fetch2(c, j + 2).start()
            for q in range(PASSES):
                @pl.when(c == (q + 1) * parts - 1)
                def _():
                    for d in range(1, cols):
                        y_out[q, d - 1] = acc[:, (d - 1) * own : d * own].astype(BF16)
                        scatter(q, d).start()

        return carry

    lax.fori_loop(0, count + DEPTH, step, 0)
    fetch_tail(0).start()
    fetch_tail(1).start()
    out[...] = jnp.zeros_like(out)

    def tail(t, carry):
        fetch_tail(t).wait()
        k, i = lax.div(t, strips), lax.rem(t, strips)
        tile = e2[lax.rem(t, 2)]
        place = at(i * strip, strip)
        for p in range(PASSES):
            out[p * lines : (p + 1) * lines, place] += dot(back[p * parts + k], tile, ((1,), (1,)))

        @pl.when(t + 2 < tails)
        def _():
            fetch_tail(t + 2).start()

        return carry

    lax.fori_loop(0, tails, tail, 0)
    for p in range(PASSES):
        for d in range(1, cols):
            scatter(p, d).wait()
            out[p * lines : (p + 1) * lines, :] += y_in[p, d - 1].astype(F32)


def shards(right_sides, eigen_basis, space_values, time_basis, time_values, noise_level):
    count, span, own = right_sides.shape
    cols, tms = lax.axis_size("col"), lax.axis_size("tm")
    lines = count * span // PASSES
    depth, width = eigen_basis.shape
    parts = min(MOST_PARTS, width // LEAST_WIDE)
    wide = width // parts
    half, quarter = wide // 2, wide // 4
    group = lines // tms
    chunks = PASSES * parts
    dma = pltpu.SemaphoreType.DMA
    vmem = pl.BlockSpec(memory_space=pltpu.VMEM)
    result = pl.pallas_call(
        functools.partial(kernel, cols, tms, span, parts),
        out_shape=jax.ShapeDtypeStruct((count * span, own), F32),
        in_specs=[pl.BlockSpec(memory_space=pltpu.SMEM), vmem, vmem, vmem, vmem]
        + [pl.BlockSpec(memory_space=pl.ANY)],
        out_specs=vmem,
        scratch_shapes=[
            pltpu.VMEM((PASSES, cols - 1, lines, own), BF16),
            pltpu.VMEM((lines, width), F32),
            pltpu.VMEM((lines, (cols - 1) * own), F32),
            pltpu.VMEM((2, cols, own, TILE), BF16),
            pltpu.VMEM((2, min(STRIP, own), wide), BF16),
            pltpu.VMEM((lines, half), F32),
            pltpu.VMEM((lines, half), BF16),
            pltpu.VMEM((chunks, lines, half), BF16),
            pltpu.VMEM((lines, quarter), F32),
            pltpu.VMEM((lines, quarter), BF16),
            pltpu.VMEM((chunks, lines, quarter), BF16),
            pltpu.VMEM((lines, quarter), BF16),
            pltpu.VMEM((chunks, tms, group, quarter), BF16),
            pltpu.VMEM((tms, group, quarter), BF16),
            pltpu.VMEM((chunks, lines, wide), BF16),
            pltpu.VMEM((PASSES, cols - 1, lines, own), BF16),
            pltpu.VMEM((PASSES, cols - 1, lines, own), BF16),
            dma((2, cols)), dma((2,)),
            dma((SEMS,)), dma((SEMS,)), dma((SEMS,)), dma((SEMS,)),
            dma((SEMS, tms - 1)), dma((SEMS, tms - 1)),
            dma((SEMS, tms - 1)), dma((SEMS, tms - 1)),
            dma((SEMS,)), dma((SEMS,)), dma((SEMS,)), dma((SEMS,)),
            dma((PASSES, cols - 1)), dma((PASSES, cols - 1)),
            dma((PASSES, cols - 1)), dma((PASSES, cols - 1)),
        ],
        compiler_params=pltpu.CompilerParams(
            collective_id=0, has_side_effects=True, vmem_limit_bytes=60 * 1024 * 1024
        ),
        cost_estimate=pl.CostEstimate(
            flops=4 * count * span * depth * width,
            bytes_accessed=4 * PASSES * depth * width,
            transcendentals=0,
        ),
    )(
        noise_level, space_values.reshape(1, -1), time_values.reshape(-1, 1), time_basis,
        right_sides.reshape(count * span, own), eigen_basis,
    )
    return result.reshape(count, span, own)


def solution(mesh):
    placed = (P(None, "tm", ("row", "col")), P("row", "col"), P("col"), P(), P(), P())
    return jax.shard_map(
        shards, mesh=mesh, in_specs=placed, out_specs=P(None, "tm", ("row", "col")), check_vma=False
    )
```
